32 devices in a mesh: lag: 16 (over z, y, x), space: 2 (over core).
Axes of the slice: x: 2, y: 2, z: 4, core: 2. Of those that a mesh axis runs over, the one named last changes fastest.
Arguments:
- ensemble: bfloat16 [16, 256, 1024], P('lag', 'space'), may hold values from -6 to 6
- slot_order: int32 [16], replicated, may hold values from 0 to 15, each once
- neighbour_shift: int32 [6, 256], P(None, 'space'), may hold values from -16 to 16, as said below
- edge_coupling: float32 [6, 256], P(None, 'space'), may hold values from 0.02 to 0.15
- observation_cells: int32 [2, 4, 32], P(None, None, 'space'), may hold values from 0 to 127
- observation_weight: float32 [2, 4, 32], P(None, None, 'space'), may hold values from 0.1 to 0.6
- observation_reading: float32 [2, 32], P(None, 'space'), may hold values from -6 to 6
- observation_variance: float32 [2, 32], replicated, may hold values from 0.25 to 2
- observation_jitter: float32 [2, 32, 1024], P(None, 'space'), may hold values from -6 to 6
Outputs:
- analysed: bfloat16 [16, 256, 1024], P('lag', 'space')
- retired: bfloat16 [2, 1024, 256], P(None, 'lag', 'space')
The draws below stay inside these ranges and needn't reach their ends.
Inputs may be any that keep to these rules, and one draw needn't show every extreme that they name: `neighbour_shift`: for each cell the 6 offsets are distinct and nonzero. `observation_cells`: observation p reads cells of the partition of 128 cells numbered p // 16.
All inputs are finite; a program needn't handle non-finite values.
Results may differ from the reference program's by a relative error of at most 0.0054.
Values may be sent and summed in bfloat16 or wider, within the bound.
A program may use at most 64 MiB of HBM per device.

```python
import math
import jax
import jax.numpy as jnp
from jax import lax

MEMBERS = 1024
CELL_DEV = 128
OBS_DEV = 16
NPTS = 4
NBRS = 6
HALO = 16
FC_STEPS = 4
CYCLES = 2
SLABS = 16
NCELLS = 256
NOBS = 32


def draw_neighbour_shift(key, part):
    scores = jax.random.randint(key, (NCELLS, 2 * HALO), 0, 1 << 20)
    scores = scores * (2 * HALO) + jnp.arange(2 * HALO, dtype=jnp.int32)[None, :]
    unused, picks = lax.top_k(scores, NBRS)
    offsets = jnp.where(picks < HALO, picks - HALO, picks - HALO + 1)
    return offsets.T.astype(jnp.int32)


def place_ends(values, own_key, smallest, largest):
    index_at = [jax.random.randint(jax.random.fold_in(own_key, axis), (), 0, length) for axis, length in enumerate(values.shape)]
    widest = values.shape.index(max(values.shape))
    beside = index_at[:widest] + [(index_at[widest] + 1) % values.shape[widest]] + index_at[widest + 1:]
    return values.at[tuple(index_at)].set(smallest).at[tuple(beside)].set(largest)


def levels(own_key, shape, pieces, smallest, high):
    level = 1.0
    for position, blocks in pieces:
        steps = jax.random.uniform(jax.random.fold_in(jax.random.fold_in(own_key, 6), position), (blocks,), jnp.float32, smallest / len(pieces), high / len(pieces))
        level = level * jnp.repeat(jnp.exp(steps), shape[position] // blocks).reshape((-1,) + (1,) * (len(shape) - 1 - position))
    return level


def noise(rng, dims, scale, limit, split=(), kind=jnp.bfloat16):
    result = scale * jax.random.normal(rng, dims, jnp.float32)
    if split:
        result = result * levels(rng, dims, split, -0.22, 0.18)
    return jnp.clip(result, -limit, limit).astype(kind)


def setup_inputs(seed: int = 0) -> dict:
    keys = jax.random.split(jax.random.key(seed), 10)
    return {
        "ensemble": noise(keys[0], (SLABS, NCELLS, MEMBERS), 1.0, 6.0, ((0, 16), (1, 2))),
        "slot_order": jax.random.permutation(keys[1], SLABS).astype(jnp.int32),
        "neighbour_shift": draw_neighbour_shift(jax.random.fold_in(keys[9], 71), 0),
        "edge_coupling": jnp.clip(jnp.exp(math.log(0.15) - 2.014903 * jax.random.uniform(keys[3], (NBRS, NCELLS), jnp.float32) ** levels(keys[3], (NBRS, NCELLS), ((1, 2),), -0.2, 0.2)), 0.02, 0.15),
        "observation_cells": place_ends(jax.random.randint(keys[4], (CYCLES, NPTS, NOBS), 0, CELL_DEV), jax.random.fold_in(keys[4], 1), 0, CELL_DEV - 1).astype(jnp.int32),
        "observation_weight": jnp.clip(0.1 + 0.5 * jax.random.uniform(keys[5], (CYCLES, NPTS, NOBS), jnp.float32) ** levels(keys[5], (CYCLES, NPTS, NOBS), ((2, 2),), -0.2, 0.2), 0.1, 0.6),
        "observation_reading": noise(keys[6], (CYCLES, NOBS), 1.0, 6.0, ((1, 2),), jnp.float32),
        "observation_variance": jnp.clip(jnp.exp(jax.random.uniform(keys[7], (CYCLES, NOBS), jnp.float32, math.log(0.25), math.log(2.0))), 0.25, 2.0),
        "observation_jitter": noise(keys[8], (CYCLES, NOBS, MEMBERS), 1.0, 6.0, ((1, 2),), jnp.float32),
    }


highest = lax.Precision.HIGHEST

def step_forward(present_state, offsets, coefficients):
    field_f = present_state.astype(jnp.float32)
    anchor = jnp.arange(field_f.shape[0], dtype=jnp.int32) + HALO
    for repeat in range(FC_STEPS):
        padded = jnp.pad(field_f, ((HALO, HALO), (0, 0)))
        accrued = jnp.zeros_like(field_f)
        for neighbour in range(NBRS):
            picked = (anchor + offsets[neighbour]).astype(jnp.int32)
            accrued = accrued + coefficients[neighbour][:, None] * (padded[picked] - field_f)
        field_f = field_f + accrued
    return field_f.astype(jnp.bfloat16)

def compute_gain_weights(predict_ahead, vertex_list, vertex_weights, observation_readings, member_variance, random_jitter):
    to_single_float = predict_ahead.astype(jnp.float32)
    first_cell = jnp.arange(NOBS, dtype=jnp.int32) // OBS_DEV * CELL_DEV
    measured = jnp.zeros((NOBS, MEMBERS), jnp.float32)
    for corner in range(NPTS):
        picked = (first_cell + vertex_list[corner]).astype(jnp.int32)
        measured = measured + vertex_weights[corner][:, None] * to_single_float[picked]
    centre = lax.optimization_barrier(jnp.mean(measured, axis=1, keepdims=True))
    spread = (measured - centre).astype(jnp.bfloat16)
    innovation = (observation_readings[:, None] + jnp.sqrt(member_variance)[:, None] * random_jitter - measured).astype(jnp.bfloat16)
    spread_f = spread.astype(jnp.float32)
    gram_matrix = jnp.dot(spread_f, spread_f.T, precision=highest) + jnp.diag((MEMBERS - 1) * member_variance)
    factor = jnp.linalg.cholesky(gram_matrix)
    solved = jax.scipy.linalg.cho_solve((factor, True), innovation.astype(jnp.float32)).astype(jnp.bfloat16)
    return jnp.dot(spread_f.T, solved.astype(jnp.float32), precision=highest).astype(jnp.bfloat16)

def assimilate_window(present_state, gain_weights):
    values = present_state.astype(jnp.float32)
    centre = lax.optimization_barrier(jnp.mean(values, axis=1, keepdims=True))
    spread = (values - centre).astype(jnp.bfloat16)
    update = jnp.dot(spread.astype(jnp.float32), gain_weights.astype(jnp.float32), precision=highest)
    return (values + update).astype(jnp.bfloat16)

def reference(ensemble, slot_order, neighbour_shift, edge_coupling, observation_cells, observation_weight, observation_reading, observation_variance, observation_jitter):
    departed = []
    for cycle_number in range(CYCLES):
        forcing_term = slot_order[(SLABS - cycle_number) % SLABS]
        target = slot_order[(SLABS - 1 - cycle_number) % SLABS]
        predict_ahead = step_forward(ensemble[forcing_term], neighbour_shift, edge_coupling)
        gain_weights = compute_gain_weights(predict_ahead, observation_cells[cycle_number], observation_weight[cycle_number], observation_reading[cycle_number], observation_variance[cycle_number], observation_jitter[cycle_number])
        refreshed_state = assimilate_window(predict_ahead, gain_weights)
        ensemble = lax.map(lambda present_state: assimilate_window(present_state, gain_weights), ensemble)
        departed.append(ensemble[target].T)
        ensemble = ensemble.at[target].set(refreshed_state)
    return (ensemble, jnp.stack(departed))
```

```python
import functools
import jax
import jax.numpy as jnp
from jax import lax
from jax.experimental import pallas as pl
from jax.experimental.pallas import tpu as pltpu
from jax.sharding import PartitionSpec as P

FC_STEPS = 4
LANES = 128
MESH = pl.DeviceIdType.MESH
VMEM_BYTES = 50 * 1024 * 1024
F32 = jnp.float32
BF16 = jnp.bfloat16


def exchange_kernel(lags, spaces, slot_ref, slab_ref, *refs):
    small_count = (len(refs) - 10) // 2
    small_in, refs = refs[:small_count], refs[small_count:]
    whole_ref, refs = refs[0], refs[1:]
    small_out, refs = refs[:small_count], refs[small_count:]
    landing, chosen, send_1, recv_1, send_2, recv_2, send_3, recv_3, sems_small = refs
    send_s, recv_s = sems_small.at[0], sems_small.at[1]
    lag, space = lax.axis_index("lag"), lax.axis_index("space")
    cells, members = slab_ref.shape
    across = members // LANES
    rows = cells * across // lags

    def place(block):
        return (
            pl.ds(pl.multiple_of((block // across) * rows, rows), rows),
            pl.ds(pl.multiple_of((block % across) * LANES, LANES), LANES),
        )

    def lag_at(step):
        return lax.rem(lag + step, lags)

    def space_at(step):
        return lax.rem(space + step, spaces)

    barrier = pltpu.get_barrier_semaphore()
    for step in range(1, lags):
        pl.semaphore_signal(barrier, inc=1, device_id=(lag_at(step), space), device_id_type=MESH)
    for step in range(1, spaces):
        pl.semaphore_signal(barrier, inc=1, device_id=(lag, space_at(step)), device_id_type=MESH)
    pl.semaphore_wait(barrier, lags - 1 + spaces - 1)

    scatter = []
    for step in range(1, lags):
        copy = pltpu.make_async_remote_copy(
            src_ref=slab_ref.at[place(lag_at(step))],
            dst_ref=landing.at[step],
            send_sem=send_1.at[step],
            recv_sem=recv_1.at[step],
            device_id=(lag_at(step), space),
            device_id_type=MESH,
        )
        copy.start()
        scatter.append(copy)
    small = []
    for step in range(1, spaces):
        for item in range(small_count):
            copy = pltpu.make_async_remote_copy(
                src_ref=small_in[item],
                dst_ref=small_out[item].at[space],
                send_sem=send_s.at[item, step],
                recv_sem=recv_s.at[item, step],
                device_id=(lag, space_at(step)),
                device_id_type=MESH,
            )
            copy.start()
            small.append(copy)
    for item in range(small_count):
        small_out[item][space] = small_in[item][...]
    source = slot_ref[0]
    block = jnp.where(lag == source, slab_ref[place(lag)], jnp.zeros((rows, LANES), BF16))
    for step in range(1, lags):
        scatter[step - 1].wait_recv()
        block = jnp.where(lag_at(lags - step) == source, landing[step], block)
    chosen[...] = block
    whole_ref[(space,) + place(lag)] = block
    gather = []
    for step in range(1, lags):
        copy = pltpu.make_async_remote_copy(
            src_ref=chosen,
            dst_ref=whole_ref.at[(space,) + place(lag)],
            send_sem=send_2.at[step],
            recv_sem=recv_2.at[step],
            device_id=(lag_at(step), space),
            device_id_type=MESH,
        )
        copy.start()
        gather.append(copy)
    forward = []
    for step in range(lags):
        if step:
            gather[step - 1].wait_recv()
        spot = (space,) + place(lag_at(lags - step) if step else lag)
        for aside in range(1, spaces):
            copy = pltpu.make_async_remote_copy(
                src_ref=whole_ref.at[spot],
                dst_ref=whole_ref.at[spot],
                send_sem=send_3.at[step, aside],
                recv_sem=recv_3.at[step, aside],
                device_id=(lag, space_at(aside)),
                device_id_type=MESH,
            )
            copy.start()
            forward.append(copy)
    for copy in scatter + gather:
        copy.wait_send()
    for copy in small + forward:
        copy.wait()


def retire_kernel(lags, slot_ref, turned_ref, out_ref, landing, send_sem, recv_sem):
    lag, space = lax.axis_index("lag"), lax.axis_index("space")
    cycles, rows = out_ref.shape[0], out_ref.shape[1]

    def lag_at(step):
        return lax.rem(lag + step, lags)

    def place(block):
        return (slice(None), pl.ds(pl.multiple_of(block * rows, rows), rows))

    barrier = pltpu.get_barrier_semaphore()
    for step in range(1, lags):
        pl.semaphore_signal(barrier, inc=1, device_id=(lag_at(step), space), device_id_type=MESH)
    pl.semaphore_wait(barrier, lags - 1)
    copies = []
    for step in range(1, lags):
        copy = pltpu.make_async_remote_copy(
            src_ref=turned_ref.at[place(lag_at(step))],
            dst_ref=landing.at[step],
            send_sem=send_sem.at[step],
            recv_sem=recv_sem.at[step],
            device_id=(lag_at(step), space),
            device_id_type=MESH,
        )
        copy.start()
        copies.append(copy)
    mine = turned_ref[place(lag)]
    blocks = [mine[cycle] for cycle in range(cycles)]
    for step in range(1, lags):
        copies[step - 1].wait_recv()
        for cycle in range(cycles):
            target = slot_ref[(lags - 1 - cycle) % lags]
            blocks[cycle] = jnp.where(
                lag_at(lags - step) == target, landing[step, cycle], blocks[cycle]
            )
    for cycle in range(cycles):
        out_ref[cycle] = blocks[cycle]
    for copy in copies:
        copy.wait_send()


def dot(a, b):
    return jnp.dot(a, b, preferred_element_type=F32)


def parts_of(value, count):
    parts = []
    for _ in range(count):
        part = value.astype(BF16)
        parts.append(part)
        value = value - part.astype(F32)
    return parts


def dot_parts(value, right, count):
    total = None
    for part in parts_of(value, count):
        term = dot(part, right)
        total = term if total is None else total + term
    return total


def iota(shape, dim):
    return lax.broadcasted_iota(jnp.int32, shape, dim)


def column_of(row):
    n = row.shape[1]
    return jnp.sum(
        jnp.where(iota((n, n), 0) == iota((n, n), 1), row, 0.0), axis=1, keepdims=True
    )


def inverse_of(gram):
    n = gram.shape[0]
    at_row, at_column = iota((n, n), 0), iota((n, n), 1)
    for k in range(n):
        pivot = 1.0 / gram[k : k + 1, k : k + 1]
        column = gram[:, k : k + 1]
        rest = jnp.where(at_column == k, 0.0, gram)
        row = jnp.where(at_column[:1] == k, 1.0, gram[k : k + 1, :]) * pivot
        gram = jnp.where(at_row == k, row, rest - column * row)
    return gram


def analysis(values, spread, solved):
    centre = jnp.mean(values, axis=1, keepdims=True)
    anomaly = (values - centre).astype(BF16)
    cross = lax.dot_general(
        anomaly, spread, (((1,), (1,)), ((), ())), preferred_element_type=F32
    )
    return (values + dot_parts(cross, solved, 2)).astype(BF16)


def smoother_kernel(
    lags, slot_ref, slab_ref, whole_ref, shift_ref, coupling_ref, cells_ref, weight_ref,
    reading_ref, jitter_ref, variance_ref, out_ref, turned_ref, matrix, forecast,
):
    lag, space = lax.axis_index("lag"), lax.axis_index("space")
    spaces, own, members = whole_ref.shape
    total = spaces * own
    cycles = variance_ref.shape[0]
    corners = cells_ref.shape[2]
    source_cell = iota((total, own), 0)
    for part in range(spaces):
        cell = iota((total, own), 1) + part * own
        kept = jnp.zeros((1, own), F32)
        entry = jnp.zeros((total, own), F32)
        for k in range(shift_ref.shape[1]):
            weight = coupling_ref[part, k : k + 1, :]
            offset = shift_ref[part, k : k + 1, :]
            entry = entry + jnp.where(source_cell - cell == offset, weight, 0.0)
            kept = kept + weight
        entry = entry + jnp.where(source_cell == cell, 1.0 - kept, 0.0)
        matrix[:, part * own : (part + 1) * own] = entry
    power = FC_STEPS
    step = matrix[...]
    while power > 1:
        step = jnp.dot(step, step, precision=lax.Precision.HIGHEST, preferred_element_type=F32)
        power //= 2
    operator = parts_of(step.T, 2)

    state = slab_ref[...]
    newest = whole_ref[...].reshape(total, members)
    for cycle in range(cycles):
        target = slot_ref[(lags - 1 - cycle) % lags]
        ahead = (dot(operator[0], newest) + dot(operator[1], newest)).astype(BF16)
        measured, readings = [], []
        for part in range(spaces):
            wanted = cells_ref.shape[3]
            hold = jnp.zeros((own, wanted), F32)
            for q in range(corners):
                hold = hold + jnp.where(
                    iota((own, wanted), 0) == cells_ref[part, cycle, q : q + 1, :],
                    weight_ref[part, cycle, q : q + 1, :],
                    0.0,
                )
            measured.append(dot_parts(hold.T, ahead[part * own : (part + 1) * own], 3))
            readings.append(
                column_of(reading_ref[part, cycle : cycle + 1, :])
                + jnp.sqrt(
                    column_of(
                        variance_ref[cycle : cycle + 1, part * wanted : (part + 1) * wanted]
                    )
                )
                * jitter_ref[part, cycle]
            )
        measured = jnp.concatenate(measured, axis=0)
        readings = jnp.concatenate(readings, axis=0)
        spread = (measured - jnp.mean(measured, axis=1, keepdims=True)).astype(BF16)
        innovation = (readings - measured).astype(BF16)
        gram = lax.dot_general(
            spread, spread, (((1,), (1,)), ((), ())), preferred_element_type=F32
        )
        n = gram.shape[0]
        gram = gram + jnp.where(
            iota((n, n), 0) == iota((n, n), 1),
            (members - 1) * variance_ref[cycle : cycle + 1, :],
            0.0,
        )
        solved = dot_parts(inverse_of(gram), innovation, 3).astype(BF16)
        updated = analysis(state.astype(F32), spread, solved)
        fresh = analysis(ahead.astype(F32), spread, solved)
        turned_ref[cycle] = updated.astype(F32).T.astype(BF16)
        forecast[...] = fresh
        fresh_own = forecast[pl.ds(pl.multiple_of(space * own, own), own), :]
        state = jnp.where(lag == target, fresh_own, updated)
        newest = fresh
    out_ref[...] = state


def on_device(
    lags, spaces, ensemble, slot_order, neighbour_shift, edge_coupling, observation_cells,
    observation_weight, observation_reading, observation_variance, observation_jitter,
):
    slab = ensemble[0]
    cells, members = slab.shape
    cycles = observation_variance.shape[0]
    across = members // LANES
    rows = cells * across // lags
    smem = pl.BlockSpec(memory_space=pltpu.SMEM)
    vmem = pl.BlockSpec(memory_space=pltpu.VMEM)
    small = [
        neighbour_shift, edge_coupling, observation_cells, observation_weight,
        observation_reading, observation_jitter,
    ]
    dma = pltpu.SemaphoreType.DMA
    whole, *gathered = pl.pallas_call(
        functools.partial(exchange_kernel, lags, spaces),
        out_shape=[jax.ShapeDtypeStruct((spaces, cells, members), BF16)]
        + [jax.ShapeDtypeStruct((spaces,) + a.shape, a.dtype) for a in small],
        in_specs=[smem] + [vmem] * (1 + len(small)),
        out_specs=[vmem] * (1 + len(small)),
        scratch_shapes=[
            pltpu.VMEM((lags, rows, LANES), BF16),
            pltpu.VMEM((rows, LANES), BF16),
            dma((lags,)), dma((lags,)), dma((lags,)), dma((lags,)),
            dma((lags, spaces)), dma((lags, spaces)),
            dma((2, len(small), spaces)),
        ],
        compiler_params=pltpu.CompilerParams(
            collective_id=0, has_side_effects=True, vmem_limit_bytes=VMEM_BYTES
        ),
        name="exchange",
    )(slot_order, slab, *small)
    analysed, turned = pl.pallas_call(
        functools.partial(smoother_kernel, lags),
        out_shape=[
            jax.ShapeDtypeStruct((cells, members), BF16),
            jax.ShapeDtypeStruct((cycles, members, cells), BF16),
        ],
        in_specs=[smem] + [vmem] * 9,
        out_specs=[vmem] * 2,
        scratch_shapes=[
            pltpu.VMEM((spaces * cells, spaces * cells), F32),
            pltpu.VMEM((spaces * cells, members), BF16),
        ],
        compiler_params=pltpu.CompilerParams(vmem_limit_bytes=VMEM_BYTES),
        name="smoother",
    )(slot_order, slab, whole, *gathered, observation_variance)
    member_rows = members // lags
    retired = pl.pallas_call(
        functools.partial(retire_kernel, lags),
        out_shape=jax.ShapeDtypeStruct((cycles, member_rows, cells), BF16),
        in_specs=[smem, vmem],
        out_specs=vmem,
        scratch_shapes=[
            pltpu.VMEM((lags, cycles, member_rows, cells), BF16),
            dma((lags,)), dma((lags,)),
        ],
        compiler_params=pltpu.CompilerParams(
            collective_id=1, has_side_effects=True, vmem_limit_bytes=VMEM_BYTES
        ),
        name="retire",
    )(slot_order, turned)
    return analysed[None], retired


def solution(mesh):
    in_specs = (
        P("lag", "space", None),
        P(),
        P(None, "space"),
        P(None, "space"),
        P(None, None, "space"),
        P(None, None, "space"),
        P(None, "space"),
        P(),
        P(None, "space", None),
    )
    out_specs = (P("lag", "space", None), P(None, "lag", "space"))
    return jax.shard_map(
        functools.partial(on_device, mesh.shape["lag"], mesh.shape["space"]),
        mesh=mesh, in_specs=in_specs, out_specs=out_specs, check_vma=False,
    )
```

```python
import functools
import jax
import jax.numpy as jnp
from jax import lax
from jax.experimental import pallas as pl
from jax.experimental.pallas import tpu as pltpu
from jax.sharding import PartitionSpec as P

FC_STEPS = 4
LANES = 128
MESH = pl.DeviceIdType.MESH
VMEM_BYTES = 50 * 1024 * 1024
F32 = jnp.float32
BF16 = jnp.bfloat16


def dot(a, b):
    return jnp.dot(a, b, preferred_element_type=F32)


def parts_of(value, count):
    parts = []
    for _ in range(count):
        part = value.astype(BF16)
        parts.append(part)
        value = value - part.astype(F32)
    return parts


def dot_parts(value, right, count):
    total = None
    for part in parts_of(value, count):
        term = dot(part, right)
        total = term if total is None else total + term
    return total


def iota(shape, dim):
    return lax.broadcasted_iota(jnp.int32, shape, dim)


def column_of(row):
    n = row.shape[1]
    return jnp.sum(
        jnp.where(iota((n, n), 0) == iota((n, n), 1), row, 0.0), axis=1, keepdims=True
    )


def inverse_of(gram):
    n = gram.shape[0]
    at_row, at_column = iota((n, n), 0), iota((n, n), 1)
    for k in range(n):
        pivot = 1.0 / gram[k : k + 1, k : k + 1]
        column = gram[:, k : k + 1]
        rest = jnp.where(at_column == k, 0.0, gram)
        row = jnp.where(at_column[:1] == k, 1.0, gram[k : k + 1, :]) * pivot
        gram = jnp.where(at_row == k, row, rest - column * row)
    return gram


def anomaly_of(values):
    centre = jnp.mean(values, axis=1, keepdims=True)
    return (values - centre).astype(BF16)


def across_members(a, b):
    return lax.dot_general(a, b, (((1,), (1,)), ((), ())), preferred_element_type=F32)


def smoother_kernel(lags, spaces, slot_ref, slab_hbm, variance_ref, *refs):
    small_in, refs = refs[:6], refs[6:]
    out_ref, retired_ref, slab_ref, whole_ref, refs = refs[0], refs[1], refs[2], refs[3], refs[4:]
    small_all, refs = refs[:6], refs[6:]
    (
        matrix, forecast, anomaly, turned, cross_out, solved_turned, landing, chosen,
        landing_turned, landing_cross, local_sem, send_l, recv_l, send_3, recv_3, send_s, recv_s,
    ) = refs
    shift_ref, coupling_ref, cells_ref, weight_ref, reading_ref, jitter_ref = small_all
    lag, space = lax.axis_index("lag"), lax.axis_index("space")
    own, members = slab_ref.shape
    total = spaces * own
    cycles = variance_ref.shape[0]
    corners, wanted = cells_ref.shape[2], cells_ref.shape[3]
    across = members // LANES
    rows = own * across // lags
    member_rows = members // lags

    def place(block):
        return (
            pl.ds(pl.multiple_of((block // across) * rows, rows), rows),
            pl.ds(pl.multiple_of((block % across) * LANES, LANES), LANES),
        )

    def member_place(block):
        return (pl.ds(pl.multiple_of(block * member_rows, member_rows), member_rows),)

    def lag_at(step):
        return lax.rem(lag + step, lags)

    def space_at(step):
        return lax.rem(space + step, spaces)

    def send_lag(kind, step, source, target):
        copy = pltpu.make_async_remote_copy(
            src_ref=source,
            dst_ref=target,
            send_sem=send_l.at[kind, step],
            recv_sem=recv_l.at[kind, step],
            device_id=(lag_at(step), space),
            device_id_type=MESH,
        )
        copy.start()
        return copy

    local = [pltpu.make_async_copy(slab_hbm, slab_ref, local_sem.at[6])]
    for item in range(6):
        local.append(
            pltpu.make_async_copy(small_in[item], small_all[item].at[space], local_sem.at[item])
        )
    for copy in local:
        copy.start()
    barrier = pltpu.get_barrier_semaphore()
    for step in range(1, lags):
        pl.semaphore_signal(barrier, inc=1, device_id=(lag_at(step), space), device_id_type=MESH)
    for step in range(1, spaces):
        pl.semaphore_signal(barrier, inc=1, device_id=(lag, space_at(step)), device_id_type=MESH)
    pl.semaphore_wait(barrier, lags - 1 + spaces - 1)

    scatter = [
        send_lag(0, step, slab_hbm.at[place(lag_at(step))], landing.at[step])
        for step in range(1, lags)
    ]
    small = []
    for step in range(1, spaces):
        for item in range(6):
            copy = pltpu.make_async_remote_copy(
                src_ref=small_in[item],
                dst_ref=small_all[item].at[space],
                send_sem=send_s.at[item, step],
                recv_sem=recv_s.at[item, step],
                device_id=(lag, space_at(step)),
                device_id_type=MESH,
            )
            copy.start()
            small.append(copy)
    for copy in local:
        copy.wait()
    for copy in small:
        copy.wait()

    source_cell = iota((total, own), 0)
    for part in range(spaces):
        cell = iota((total, own), 1) + part * own
        kept = jnp.zeros((1, own), F32)
        entry = jnp.zeros((total, own), F32)
        for k in range(shift_ref.shape[1]):
            weight = coupling_ref[part, k : k + 1, :]
            offset = shift_ref[part, k : k + 1, :]
            entry = entry + jnp.where(source_cell - cell == offset, weight, 0.0)
            kept = kept + weight
        entry = entry + jnp.where(source_cell == cell, 1.0 - kept, 0.0)
        matrix[:, part * own : (part + 1) * own] = entry
    power = FC_STEPS
    one = matrix[...]
    while power > 1:
        one = jnp.dot(one, one, precision=lax.Precision.HIGHEST, preferred_element_type=F32)
        power //= 2
    operator = parts_of(one.T, 2)
    holds, readings = [], []
    for cycle in range(cycles):
        hold_cycle, reading_cycle = [], []
        for part in range(spaces):
            hold = jnp.zeros((own, wanted), F32)
            for q in range(corners):
                hold = hold + jnp.where(
                    iota((own, wanted), 0) == cells_ref[part, cycle, q : q + 1, :],
                    weight_ref[part, cycle, q : q + 1, :],
                    0.0,
                )
            hold_cycle.append(hold.T)
            variance = variance_ref[cycle : cycle + 1, part * wanted : (part + 1) * wanted]
            reading_cycle.append(
                column_of(reading_ref[part, cycle : cycle + 1, :])
                + jnp.sqrt(column_of(variance)) * jitter_ref[part, cycle]
            )
        holds.append(hold_cycle)
        readings.append(jnp.concatenate(reading_cycle, axis=0))

    source = slot_ref[0]
    block = jnp.where(lag == source, slab_ref[place(lag)], jnp.zeros((rows, LANES), BF16))
    for step in range(1, lags):
        scatter[step - 1].wait_recv()
        block = jnp.where(lag_at(lags - step) == source, landing[step], block)
    chosen[...] = block
    whole_ref[(space,) + place(lag)] = block
    gather = [
        send_lag(1, step, chosen, whole_ref.at[(space,) + place(lag)]) for step in range(1, lags)
    ]
    anomaly[...] = anomaly_of(slab_ref[...].astype(F32))
    forward = []
    for step in range(lags):
        if step:
            gather[step - 1].wait_recv()
        spot = (space,) + place(lag_at(lags - step) if step else lag)
        for aside in range(1, spaces):
            copy = pltpu.make_async_remote_copy(
                src_ref=whole_ref.at[spot],
                dst_ref=whole_ref.at[spot],
                send_sem=send_3.at[step, aside],
                recv_sem=recv_3.at[step, aside],
                device_id=(lag, space_at(aside)),
                device_id_type=MESH,
            )
            copy.start()
            forward.append(copy)
    for copy in forward:
        copy.wait_recv()

    def observed(cycle, ahead):
        measured = jnp.concatenate(
            [
                dot_parts(holds[cycle][part], ahead[part * own : (part + 1) * own], 3)
                for part in range(spaces)
            ],
            axis=0,
        )
        return anomaly_of(measured), (readings[cycle] - measured).astype(BF16)

    def solve(cycle, spread, innovation):
        gram = across_members(spread, spread)
        n = gram.shape[0]
        gram = gram + jnp.where(
            iota((n, n), 0) == iota((n, n), 1),
            (members - 1) * variance_ref[cycle : cycle + 1, :],
            0.0,
        )
        return dot_parts(inverse_of(gram), innovation, 3).astype(BF16)

    def own_rows(value):
        forecast[...] = value
        return forecast[pl.ds(pl.multiple_of(space * own, own), own), :]

    target_0, target_1 = slot_ref[lags - 1], slot_ref[lags - 2]

    newest = whole_ref[...].reshape(total, members)
    ahead = (dot(operator[0], newest) + dot(operator[1], newest)).astype(BF16)
    spread, innovation = observed(0, ahead)
    cross = across_members(anomaly[...], spread)
    ahead_f = ahead.astype(F32)
    cross_ahead = across_members(anomaly_of(ahead_f), spread)
    solved = solve(0, spread, innovation)
    updated = slab_ref[...].astype(F32) + dot_parts(cross, solved, 2)
    turned[...] = updated.T.astype(BF16)
    exchanged = [
        send_lag(2, step, turned.at[member_place(lag_at(step))], landing_turned.at[step])
        for step in range(1, lags)
    ]
    newest = (ahead_f + dot_parts(cross_ahead, solved, 2)).astype(BF16)
    state = jnp.where(lag == target_0, own_rows(newest), updated.astype(BF16)).astype(F32)

    ahead = (dot(operator[0], newest) + dot(operator[1], newest)).astype(BF16)
    spread, innovation = observed(1, ahead)
    cross = across_members(anomaly_of(state), spread)
    cross_out[...] = cross.T.astype(BF16)
    crosses = [
        send_lag(3, step, cross_out, landing_cross.at[step]) for step in range(1, lags)
    ]
    ahead_own = own_rows(ahead).astype(F32)
    cross_ahead = across_members(anomaly_of(ahead_own), spread)
    solved = solve(1, spread, innovation)
    base = jnp.where(lag == target_1, ahead_own, state)
    cross = jnp.where(lag == target_1, cross_ahead, cross)
    out_ref[...] = (base + dot_parts(cross, solved, 2)).astype(BF16)
    solved_turned[...] = solved.astype(F32).T

    first = turned[member_place(lag)]
    second = first
    for step in range(1, lags):
        exchanged[step - 1].wait_recv()
        sender = lag_at(lags - step)
        first = jnp.where(sender == target_0, landing_turned[step], first)
        second = jnp.where(sender == target_1, landing_turned[step], second)
    retired_ref[0] = first
    cross_turned = cross_out[...]
    for step in range(1, lags):
        crosses[step - 1].wait_recv()
        sender = lag_at(lags - step)
        cross_turned = jnp.where(sender == target_1, landing_cross[step], cross_turned)
    mine = solved_turned[member_place(lag)].astype(BF16)
    retired_ref[1] = (second.astype(F32) + dot(mine, cross_turned)).astype(BF16)
    for copy in scatter + gather + forward + exchanged + crosses:
        copy.wait_send()


def on_device(
    lags, spaces, ensemble, slot_order, neighbour_shift, edge_coupling, observation_cells,
    observation_weight, observation_reading, observation_variance, observation_jitter,
):
    slab = ensemble[0]
    own, members = slab.shape
    cycles, count = observation_variance.shape
    rows = own * (members // LANES) // lags
    member_rows = members // lags
    total = spaces * own
    smem = pl.BlockSpec(memory_space=pltpu.SMEM)
    vmem = pl.BlockSpec(memory_space=pltpu.VMEM)
    hbm = pl.BlockSpec(memory_space=pltpu.HBM)
    small = [
        neighbour_shift, edge_coupling, observation_cells, observation_weight,
        observation_reading, observation_jitter,
    ]
    dma = pltpu.SemaphoreType.DMA
    analysed, retired = pl.pallas_call(
        functools.partial(smoother_kernel, lags, spaces),
        out_shape=[
            jax.ShapeDtypeStruct((own, members), BF16),
            jax.ShapeDtypeStruct((cycles, member_rows, own), BF16),
        ],
        in_specs=[smem, hbm, vmem] + [hbm] * len(small),
        out_specs=[vmem] * 2,
        scratch_shapes=[
            pltpu.VMEM((own, members), BF16),
            pltpu.VMEM((spaces, own, members), BF16),
        ]
        + [pltpu.VMEM((spaces,) + a.shape, a.dtype) for a in small]
        + [
            pltpu.VMEM((total, total), F32),
            pltpu.VMEM((total, members), BF16),
            pltpu.VMEM((own, members), BF16),
            pltpu.VMEM((members, own), BF16),
            pltpu.VMEM((count, own), BF16),
            pltpu.VMEM((members, count), F32),
            pltpu.VMEM((lags, rows, LANES), BF16),
            pltpu.VMEM((rows, LANES), BF16),
            pltpu.VMEM((lags, member_rows, own), BF16),
            pltpu.VMEM((lags, count, own), BF16),
            dma((7,)),
            dma((4, lags)), dma((4, lags)),
            dma((lags, spaces)), dma((lags, spaces)),
            dma((6, spaces)), dma((6, spaces)),
        ],
        compiler_params=pltpu.CompilerParams(
            collective_id=0, has_side_effects=True, vmem_limit_bytes=VMEM_BYTES
        ),
        name="smoother",
    )(slot_order, slab, observation_variance, *small)
    return analysed[None], retired


def solution(mesh):
    in_specs = (
        P("lag", "space", None),
        P(),
        P(None, "space"),
        P(None, "space"),
        P(None, None, "space"),
        P(None, None, "space"),
        P(None, "space"),
        P(),
        P(None, "space", None),
    )
    out_specs = (P("lag", "space", None), P(None, "lag", "space"))
    return jax.shard_map(
        functools.partial(on_device, mesh.shape["lag"], mesh.shape["space"]),
        mesh=mesh, in_specs=in_specs, out_specs=out_specs, check_vma=False,
    )
```

```python
import functools
import jax
import jax.numpy as jnp
from jax import lax
from jax.experimental import pallas as pl
from jax.experimental.pallas import tpu as pltpu
from jax.sharding import PartitionSpec as P

FC_STEPS = 4
LANES = 128
MESH = pl.DeviceIdType.MESH
VMEM_BYTES = 64 * 1024 * 1024
F32 = jnp.float32
BF16 = jnp.bfloat16


def dot(a, b):
    return jnp.dot(a, b, preferred_element_type=F32)


def parts_of(value, count):
    parts = []
    for _ in range(count):
        part = value.astype(BF16)
        parts.append(part)
        value = value - part.astype(F32)
    return parts


def dot_parts(value, right, count):
    total = None
    for part in parts_of(value, count):
        term = dot(part, right)
        total = term if total is None else total + term
    return total


def iota(shape, dim):
    return lax.broadcasted_iota(jnp.int32, shape, dim)


def column_of(row):
    n = row.shape[1]
    return jnp.sum(
        jnp.where(iota((n, n), 0) == iota((n, n), 1), row, 0.0), axis=1, keepdims=True
    )


def inverse_of(gram):
    n = gram.shape[0]
    at_row, at_column = iota((n, n), 0), iota((n, n), 1)
    line = at_column[:1]
    for k in range(0, n, 2):
        left = jnp.broadcast_to(gram[:, k : k + 1], (n, n))
        right = jnp.broadcast_to(gram[:, k + 1 : k + 2], (n, n))
        a, b, d = left[k : k + 1], left[k + 1 : k + 2], right[k + 1 : k + 2]
        scale = 1.0 / (a * d - b * b)
        pivots = (line == k) | (line == k + 1)
        upper = jnp.where(pivots, jnp.where(line == k, 1.0, 0.0), gram[k : k + 1])
        lower = jnp.where(pivots, jnp.where(line == k, 0.0, 1.0), gram[k + 1 : k + 2])
        first = (d * upper - b * lower) * scale
        second = (a * lower - b * upper) * scale
        rest = jnp.where((at_column == k) | (at_column == k + 1), 0.0, gram)
        rest = rest - left * first - right * second
        gram = jnp.where(at_row == k, first, jnp.where(at_row == k + 1, second, rest))
    return gram


def anomaly_of(values):
    centre = jnp.mean(values, axis=1, keepdims=True)
    return (values - centre).astype(BF16)


def across_members(a, b):
    return lax.dot_general(a, b, (((1,), (1,)), ((), ())), preferred_element_type=F32)


def smoother_kernel(lags, spaces, slot_ref, slab_hbm, variance_hbm, *refs):
    small_in, refs = refs[:6], refs[6:]
    out_ref, retired_ref, slab_ref, whole_ref, refs = refs[0], refs[1], refs[2], refs[3], refs[4:]
    small_all, refs = refs[:6], refs[6:]
    (
        variance_ref, matrix, forecast, anomaly, turned, cross_out, solved_turned, landing, chosen,
        landing_turned, landing_cross, local_sem, send_l, recv_l, send_3, recv_3, send_s, recv_s,
    ) = refs
    shift_ref, coupling_ref, cells_ref, weight_ref, reading_ref, jitter_ref = small_all
    lag, space = lax.axis_index("lag"), lax.axis_index("space")
    own, members = slab_ref.shape
    total = spaces * own
    cycles = variance_ref.shape[0]
    corners, wanted = cells_ref.shape[2], cells_ref.shape[3]
    across = members // LANES
    rows = own * across // lags
    member_rows = members // lags

    def place(block):
        return (
            pl.ds(pl.multiple_of((block // across) * rows, rows), rows),
            pl.ds(pl.multiple_of((block % across) * LANES, LANES), LANES),
        )

    def member_place(block):
        return (pl.ds(pl.multiple_of(block * member_rows, member_rows), member_rows),)

    def lag_at(step):
        return lax.rem(lag + step, lags)

    def space_at(step):
        return lax.rem(space + step, spaces)

    def send_lag(kind, step, source, target):
        copy = pltpu.make_async_remote_copy(
            src_ref=source,
            dst_ref=target,
            send_sem=send_l.at[kind, step],
            recv_sem=recv_l.at[kind, step],
            device_id=(lag_at(step), space),
            device_id_type=MESH,
        )
        copy.start()
        return copy

    local = [
        pltpu.make_async_copy(slab_hbm, slab_ref, local_sem.at[6]),
        pltpu.make_async_copy(variance_hbm, variance_ref, local_sem.at[7]),
    ]
    for item in range(6):
        local.append(
            pltpu.make_async_copy(small_in[item], small_all[item].at[space], local_sem.at[item])
        )
    for copy in local:
        copy.start()
    barrier = pltpu.get_barrier_semaphore()
    for step in range(1, lags):
        pl.semaphore_signal(barrier, inc=1, device_id=(lag_at(step), space), device_id_type=MESH)
    for step in range(1, spaces):
        pl.semaphore_signal(barrier, inc=1, device_id=(lag, space_at(step)), device_id_type=MESH)
    pl.semaphore_wait(barrier, lags - 1 + spaces - 1)

    scatter = [
        send_lag(0, step, slab_hbm.at[place(lag_at(step))], landing.at[step])
        for step in range(1, lags)
    ]
    small = []
    for step in range(1, spaces):
        for item in range(6):
            copy = pltpu.make_async_remote_copy(
                src_ref=small_in[item],
                dst_ref=small_all[item].at[space],
                send_sem=send_s.at[item, step],
                recv_sem=recv_s.at[item, step],
                device_id=(lag, space_at(step)),
                device_id_type=MESH,
            )
            copy.start()
            small.append(copy)
    for copy in local:
        copy.wait()
    for copy in small:
        copy.wait()

    source_cell = iota((total, own), 0)
    for part in range(spaces):
        cell = iota((total, own), 1) + part * own
        kept = jnp.zeros((1, own), F32)
        entry = jnp.zeros((total, own), F32)
        for k in range(shift_ref.shape[1]):
            weight = coupling_ref[part, k : k + 1, :]
            offset = shift_ref[part, k : k + 1, :]
            entry = entry + jnp.where(source_cell - cell == offset, weight, 0.0)
            kept = kept + weight
        entry = entry + jnp.where(source_cell == cell, 1.0 - kept, 0.0)
        matrix[:, part * own : (part + 1) * own] = entry
    power = FC_STEPS
    one = matrix[...]
    while power > 1:
        one = jnp.dot(one, one, precision=lax.Precision.HIGHEST, preferred_element_type=F32)
        power //= 2
    operator = parts_of(one.T, 2)
    holds, readings = [], []
    for cycle in range(cycles):
        hold_cycle, reading_cycle = [], []
        for part in range(spaces):
            hold = jnp.zeros((own, wanted), F32)
            for q in range(corners):
                hold = hold + jnp.where(
                    iota((own, wanted), 0) == cells_ref[part, cycle, q : q + 1, :],
                    weight_ref[part, cycle, q : q + 1, :],
                    0.0,
                )
            hold_cycle.append(hold.T)
            variance = variance_ref[cycle : cycle + 1, part * wanted : (part + 1) * wanted]
            reading_cycle.append(
                column_of(reading_ref[part, cycle : cycle + 1, :])
                + jnp.sqrt(column_of(variance)) * jitter_ref[part, cycle]
            )
        holds.append(hold_cycle)
        readings.append(jnp.concatenate(reading_cycle, axis=0))

    source = slot_ref[0]
    block = jnp.where(lag == source, slab_ref[place(lag)], jnp.zeros((rows, LANES), BF16))
    for step in range(1, lags):
        scatter[step - 1].wait_recv()
        block = jnp.where(lag_at(lags - step) == source, landing[step], block)
    chosen[...] = block
    whole_ref[(space,) + place(lag)] = block
    gather = [
        send_lag(1, step, chosen, whole_ref.at[(space,) + place(lag)]) for step in range(1, lags)
    ]
    anomaly[...] = anomaly_of(slab_ref[...].astype(F32))
    forward = []
    for step in range(lags):
        if step:
            gather[step - 1].wait_recv()
        spot = (space,) + place(lag_at(lags - step) if step else lag)
        for aside in range(1, spaces):
            copy = pltpu.make_async_remote_copy(
                src_ref=whole_ref.at[spot],
                dst_ref=whole_ref.at[spot],
                send_sem=send_3.at[step, aside],
                recv_sem=recv_3.at[step, aside],
                device_id=(lag, space_at(aside)),
                device_id_type=MESH,
            )
            copy.start()
            forward.append(copy)
    for copy in forward:
        copy.wait_recv()

    def observed(cycle, ahead):
        measured = jnp.concatenate(
            [
                dot_parts(holds[cycle][part], ahead[part * own : (part + 1) * own], 3)
                for part in range(spaces)
            ],
            axis=0,
        )
        return anomaly_of(measured), (readings[cycle] - measured).astype(BF16)

    def solve(cycle, spread, innovation):
        gram = across_members(spread, spread)
        n = gram.shape[0]
        gram = gram + jnp.where(
            iota((n, n), 0) == iota((n, n), 1),
            (members - 1) * variance_ref[cycle : cycle + 1, :],
            0.0,
        )
        return dot_parts(inverse_of(gram), innovation, 3).astype(BF16)

    def own_rows(value):
        forecast[...] = value
        return forecast[pl.ds(pl.multiple_of(space * own, own), own), :]

    target_0, target_1 = slot_ref[lags - 1], slot_ref[lags - 2]

    newest = whole_ref[...].reshape(total, members)
    ahead = (dot(operator[0], newest) + dot(operator[1], newest)).astype(BF16)
    spread, innovation = observed(0, ahead)
    cross = across_members(anomaly[...], spread)
    ahead_f = ahead.astype(F32)
    cross_ahead = across_members(anomaly_of(ahead_f), spread)
    solved = solve(0, spread, innovation)
    updated = slab_ref[...].astype(F32) + dot_parts(cross, solved, 2)
    turned[...] = updated.T.astype(BF16)
    exchanged = [
        send_lag(2, step, turned.at[member_place(lag_at(step))], landing_turned.at[step])
        for step in range(1, lags)
    ]
    newest = (ahead_f + dot_parts(cross_ahead, solved, 2)).astype(BF16)
    state = jnp.where(lag == target_0, own_rows(newest), updated.astype(BF16)).astype(F32)

    ahead = (dot(operator[0], newest) + dot(operator[1], newest)).astype(BF16)
    spread, innovation = observed(1, ahead)
    cross = across_members(anomaly_of(state), spread)
    cross_out[...] = cross.T.astype(BF16)
    crosses = [
        send_lag(3, step, cross_out, landing_cross.at[step]) for step in range(1, lags)
    ]
    ahead_own = own_rows(ahead).astype(F32)
    cross_ahead = across_members(anomaly_of(ahead_own), spread)
    solved = solve(1, spread, innovation)
    base = jnp.where(lag == target_1, ahead_own, state)
    cross = jnp.where(lag == target_1, cross_ahead, cross)
    out_ref[...] = (base + dot_parts(cross, solved, 2)).astype(BF16)
    solved_turned[...] = solved.astype(F32).T

    first = turned[member_place(lag)]
    second = first
    for step in range(1, lags):
        exchanged[step - 1].wait_recv()
        sender = lag_at(lags - step)
        first = jnp.where(sender == target_0, landing_turned[step], first)
        second = jnp.where(sender == target_1, landing_turned[step], second)
    retired_ref[0] = first
    cross_turned = cross_out[...]
    for step in range(1, lags):
        crosses[step - 1].wait_recv()
        sender = lag_at(lags - step)
        cross_turned = jnp.where(sender == target_1, landing_cross[step], cross_turned)
    mine = solved_turned[member_place(lag)].astype(BF16)
    retired_ref[1] = (second.astype(F32) + dot(mine, cross_turned)).astype(BF16)
    for copy in scatter + gather + forward + exchanged + crosses:
        copy.wait_send()


def on_device(
    lags, spaces, ensemble, slot_order, neighbour_shift, edge_coupling, observation_cells,
    observation_weight, observation_reading, observation_variance, observation_jitter,
):
    slab = ensemble[0]
    own, members = slab.shape
    cycles, count = observation_variance.shape
    rows = own * (members // LANES) // lags
    member_rows = members // lags
    total = spaces * own
    smem = pl.BlockSpec(memory_space=pltpu.SMEM)
    vmem = pl.BlockSpec(memory_space=pltpu.VMEM)
    hbm = pl.BlockSpec(memory_space=pltpu.HBM)
    small = [
        neighbour_shift, edge_coupling, observation_cells, observation_weight,
        observation_reading, observation_jitter,
    ]
    dma = pltpu.SemaphoreType.DMA
    analysed, retired = pl.pallas_call(
        functools.partial(smoother_kernel, lags, spaces),
        out_shape=[
            jax.ShapeDtypeStruct((own, members), BF16),
            jax.ShapeDtypeStruct((cycles, member_rows, own), BF16),
        ],
        in_specs=[smem, hbm, hbm] + [hbm] * len(small),
        out_specs=[vmem] * 2,
        scratch_shapes=[
            pltpu.VMEM((own, members), BF16),
            pltpu.VMEM((spaces, own, members), BF16),
        ]
        + [pltpu.VMEM((spaces,) + a.shape, a.dtype) for a in small]
        + [
            pltpu.VMEM((cycles, count), F32),
            pltpu.VMEM((total, total), F32),
            pltpu.VMEM((total, members), BF16),
            pltpu.VMEM((own, members), BF16),
            pltpu.VMEM((members, own), BF16),
            pltpu.VMEM((count, own), BF16),
            pltpu.VMEM((members, count), F32),
            pltpu.VMEM((lags, rows, LANES), BF16),
            pltpu.VMEM((rows, LANES), BF16),
            pltpu.VMEM((lags, member_rows, own), BF16),
            pltpu.VMEM((lags, count, own), BF16),
            dma((8,)),
            dma((4, lags)), dma((4, lags)),
            dma((lags, spaces)), dma((lags, spaces)),
            dma((6, spaces)), dma((6, spaces)),
        ],
        compiler_params=pltpu.CompilerParams(
            collective_id=0, has_side_effects=True, vmem_limit_bytes=VMEM_BYTES
        ),
        name="smoother",
    )(slot_order, slab, observation_variance, *small)
    return analysed[None], retired


def solution(mesh):
    in_specs = (
        P("lag", "space", None),
        P(),
        P(None, "space"),
        P(None, "space"),
        P(None, None, "space"),
        P(None, None, "space"),
        P(None, "space"),
        P(),
        P(None, "space", None),
    )
    out_specs = (P("lag", "space", None), P(None, "lag", "space"))
    return jax.shard_map(
        functools.partial(on_device, mesh.shape["lag"], mesh.shape["space"]),
        mesh=mesh, in_specs=in_specs, out_specs=out_specs, check_vma=False,
    )
```

```python
import functools
import jax
import jax.numpy as jnp
from jax import lax
from jax.experimental import pallas as pl
from jax.experimental.pallas import tpu as pltpu
from jax.sharding import PartitionSpec as P

FC_STEPS = 4
MESH = pl.DeviceIdType.MESH
VMEM_BYTES = 64 * 1024 * 1024
F32 = jnp.float32
BF16 = jnp.bfloat16


def dot(a, b):
    return jnp.dot(a, b, preferred_element_type=F32)


def parts_of(value, count):
    parts = []
    for _ in range(count):
        part = value.astype(BF16)
        parts.append(part)
        value = value - part.astype(F32)
    return parts


def dot_parts(value, right, count):
    total = None
    for part in parts_of(value, count):
        term = dot(part, right)
        total = term if total is None else total + term
    return total


def iota(shape, dim):
    return lax.broadcasted_iota(jnp.int32, shape, dim)


def column_of(row):
    n = row.shape[1]
    return jnp.sum(
        jnp.where(iota((n, n), 0) == iota((n, n), 1), row, 0.0), axis=1, keepdims=True
    )


def inverse_of(gram):
    n = gram.shape[0]
    at_row, at_column = iota((n, n), 0), iota((n, n), 1)
    line = at_column[:1]
    for k in range(0, n, 2):
        left = jnp.broadcast_to(gram[:, k : k + 1], (n, n))
        right = jnp.broadcast_to(gram[:, k + 1 : k + 2], (n, n))
        a, b, d = left[k : k + 1], left[k + 1 : k + 2], right[k + 1 : k + 2]
        scale = 1.0 / (a * d - b * b)
        pivots = (line == k) | (line == k + 1)
        upper = jnp.where(pivots, jnp.where(line == k, 1.0, 0.0), gram[k : k + 1])
        lower = jnp.where(pivots, jnp.where(line == k, 0.0, 1.0), gram[k + 1 : k + 2])
        first = (d * upper - b * lower) * scale
        second = (a * lower - b * upper) * scale
        rest = jnp.where((at_column == k) | (at_column == k + 1), 0.0, gram)
        rest = rest - left * first - right * second
        gram = jnp.where(at_row == k, first, jnp.where(at_row == k + 1, second, rest))
    return gram


def anomaly_of(values):
    centre = jnp.mean(values, axis=1, keepdims=True)
    return (values - centre).astype(BF16)


def across_members(a, b):
    return lax.dot_general(a, b, (((1,), (1,)), ((), ())), preferred_element_type=F32)


def smoother_kernel(lags, spaces, slot_ref, slab_hbm, variance_hbm, *refs):
    small_in, refs = refs[:6], refs[6:]
    out_ref, retired_ref, slab_ref, whole_ref, refs = refs[0], refs[1], refs[2], refs[3], refs[4:]
    small_all, refs = refs[:6], refs[6:]
    (
        variance_ref, matrix, forecast, anomaly, turned, cross_out, solved_turned, landing, chosen,
        landing_cross, local_sem, send_l, recv_l, send_3, recv_3, send_s, recv_s,
    ) = refs
    shift_ref, coupling_ref, cells_ref, weight_ref, reading_ref, jitter_ref = small_all
    lag, space = lax.axis_index("lag"), lax.axis_index("space")
    own, members = slab_ref.shape
    total = spaces * own
    cycles = variance_ref.shape[0]
    corners, wanted = cells_ref.shape[2], cells_ref.shape[3]
    member_rows = members // lags

    def member_place(block):
        return pl.ds(pl.multiple_of(block * member_rows, member_rows), member_rows)

    def lag_at(step):
        return lax.rem(lag + step, lags)

    def space_at(step):
        return lax.rem(space + step, spaces)

    def send_lag(kind, step, source, target):
        copy = pltpu.make_async_remote_copy(
            src_ref=source,
            dst_ref=target,
            send_sem=send_l.at[kind, step],
            recv_sem=recv_l.at[kind, step],
            device_id=(lag_at(step), space),
            device_id_type=MESH,
        )
        copy.start()
        return copy

    local = [
        pltpu.make_async_copy(slab_hbm, slab_ref, local_sem.at[6]),
        pltpu.make_async_copy(variance_hbm, variance_ref, local_sem.at[7]),
    ]
    for item in range(6):
        local.append(
            pltpu.make_async_copy(small_in[item], small_all[item].at[space], local_sem.at[item])
        )
    for copy in local:
        copy.start()
    barrier = pltpu.get_barrier_semaphore()
    for step in range(1, lags):
        pl.semaphore_signal(barrier, inc=1, device_id=(lag_at(step), space), device_id_type=MESH)
    for step in range(1, spaces):
        pl.semaphore_signal(barrier, inc=1, device_id=(lag, space_at(step)), device_id_type=MESH)
    local[0].wait()
    turned[...] = slab_ref[...].astype(F32).T.astype(BF16)
    pl.semaphore_wait(barrier, lags - 1 + spaces - 1)

    scatter = [
        send_lag(0, step, turned.at[member_place(lag_at(step))], landing.at[step])
        for step in range(1, lags)
    ]
    small = []
    for step in range(1, spaces):
        for item in range(6):
            copy = pltpu.make_async_remote_copy(
                src_ref=small_in[item],
                dst_ref=small_all[item].at[space],
                send_sem=send_s.at[item, step],
                recv_sem=recv_s.at[item, step],
                device_id=(lag, space_at(step)),
                device_id_type=MESH,
            )
            copy.start()
            small.append(copy)
    for copy in local[1:]:
        copy.wait()
    for copy in small:
        copy.wait()

    source_cell = iota((total, own), 0)
    for part in range(spaces):
        cell = iota((total, own), 1) + part * own
        kept = jnp.zeros((1, own), F32)
        entry = jnp.zeros((total, own), F32)
        for k in range(shift_ref.shape[1]):
            weight = coupling_ref[part, k : k + 1, :]
            offset = shift_ref[part, k : k + 1, :]
            entry = entry + jnp.where(source_cell - cell == offset, weight, 0.0)
            kept = kept + weight
        entry = entry + jnp.where(source_cell == cell, 1.0 - kept, 0.0)
        matrix[:, part * own : (part + 1) * own] = entry
    power = FC_STEPS
    one = matrix[...]
    while power > 1:
        one = jnp.dot(one, one, precision=lax.Precision.HIGHEST, preferred_element_type=F32)
        power //= 2
    operator = parts_of(one.T, 2)
    holds, readings = [], []
    for cycle in range(cycles):
        hold_cycle, reading_cycle = [], []
        for part in range(spaces):
            hold = jnp.zeros((own, wanted), F32)
            for q in range(corners):
                hold = hold + jnp.where(
                    iota((own, wanted), 0) == cells_ref[part, cycle, q : q + 1, :],
                    weight_ref[part, cycle, q : q + 1, :],
                    0.0,
                )
            hold_cycle.append(hold.T)
            variance = variance_ref[cycle : cycle + 1, part * wanted : (part + 1) * wanted]
            reading_cycle.append(
                column_of(reading_ref[part, cycle : cycle + 1, :])
                + jnp.sqrt(column_of(variance)) * jitter_ref[part, cycle]
            )
        holds.append(hold_cycle)
        readings.append(jnp.concatenate(reading_cycle, axis=0))

    source, target_0, target_1 = slot_ref[0], slot_ref[lags - 1], slot_ref[lags - 2]
    mine = turned[member_place(lag)]
    block = mine
    for step in range(1, lags):
        scatter[step - 1].wait_recv()
        block = jnp.where(lag_at(lags - step) == source, landing[step], block)
    chosen[...] = block
    whole_ref[space, member_place(lag)] = block
    gather = [
        send_lag(1, step, chosen, whole_ref.at[space, member_place(lag)])
        for step in range(1, lags)
    ]
    first, second = mine, mine
    for step in range(1, lags):
        sender = lag_at(lags - step)
        first = jnp.where(sender == target_0, landing[step], first)
        second = jnp.where(sender == target_1, landing[step], second)
    anomaly[...] = anomaly_of(slab_ref[...].astype(F32))
    forward = []
    for step in range(lags):
        if step:
            gather[step - 1].wait_recv()
        spot = (space, member_place(lag_at(lags - step) if step else lag))
        for aside in range(1, spaces):
            copy = pltpu.make_async_remote_copy(
                src_ref=whole_ref.at[spot],
                dst_ref=whole_ref.at[spot],
                send_sem=send_3.at[step, aside],
                recv_sem=recv_3.at[step, aside],
                device_id=(lag, space_at(aside)),
                device_id_type=MESH,
            )
            copy.start()
            forward.append(copy)
    for copy in forward:
        copy.wait_recv()

    def observed(cycle, ahead):
        measured = jnp.concatenate(
            [
                dot_parts(holds[cycle][part], ahead[part * own : (part + 1) * own], 3)
                for part in range(spaces)
            ],
            axis=0,
        )
        return anomaly_of(measured), (readings[cycle] - measured).astype(BF16)

    def solve(cycle, spread, innovation):
        gram = across_members(spread, spread)
        n = gram.shape[0]
        gram = gram + jnp.where(
            iota((n, n), 0) == iota((n, n), 1),
            (members - 1) * variance_ref[cycle : cycle + 1, :],
            0.0,
        )
        return dot_parts(inverse_of(gram), innovation, 3).astype(BF16)

    def own_rows(value):
        forecast[...] = value
        return forecast[pl.ds(pl.multiple_of(space * own, own), own), :]

    def send_cross(cycle, cross):
        cross_out[cycle] = cross.T.astype(BF16)
        return [
            send_lag(2 + cycle, step, cross_out.at[cycle], landing_cross.at[cycle, step])
            for step in range(1, lags)
        ]

    def chosen_cross(cycle, target):
        value = cross_out[cycle]
        for step in range(1, lags):
            value = jnp.where(lag_at(lags - step) == target, landing_cross[cycle, step], value)
        return value

    def retire(cycle, values, solved, cross):
        solved_turned[cycle] = solved.astype(F32).T
        weights = solved_turned[cycle, member_place(lag)].astype(BF16)
        return (values.astype(F32) + dot(weights, cross)).astype(BF16)

    newest = jnp.concatenate([whole_ref[part] for part in range(spaces)], axis=1)
    ahead = (across_members(operator[0], newest) + across_members(operator[1], newest)).astype(BF16)
    spread, innovation = observed(0, ahead)
    cross = across_members(anomaly[...], spread)
    crosses = send_cross(0, cross)
    ahead_f = ahead.astype(F32)
    cross_ahead = across_members(anomaly_of(ahead_f), spread)
    solved_0 = solve(0, spread, innovation)
    newest = (ahead_f + dot_parts(cross_ahead, solved_0, 2)).astype(BF16)
    updated = (slab_ref[...].astype(F32) + dot_parts(cross, solved_0, 2)).astype(BF16)
    state = jnp.where(lag == target_0, own_rows(newest), updated).astype(F32)

    ahead = (dot(operator[0], newest) + dot(operator[1], newest)).astype(BF16)
    spread, innovation = observed(1, ahead)
    cross = across_members(anomaly_of(state), spread)
    crosses_1 = send_cross(1, cross)
    ahead_own = own_rows(ahead).astype(F32)
    cross_ahead = across_members(anomaly_of(ahead_own), spread)
    solved_1 = solve(1, spread, innovation)
    base = jnp.where(lag == target_1, ahead_own, state)
    cross = jnp.where(lag == target_1, cross_ahead, cross)
    out_ref[...] = (base + dot_parts(cross, solved_1, 2)).astype(BF16)

    for copy in crosses:
        copy.wait_recv()
    retired_ref[0] = retire(0, first, solved_0, chosen_cross(0, target_0))
    second = retire(0, second, solved_0, chosen_cross(0, target_1))
    for copy in crosses_1:
        copy.wait_recv()
    retired_ref[1] = retire(1, second, solved_1, chosen_cross(1, target_1))
    for copy in scatter + gather + forward + crosses + crosses_1:
        copy.wait_send()


def on_device(
    lags, spaces, ensemble, slot_order, neighbour_shift, edge_coupling, observation_cells,
    observation_weight, observation_reading, observation_variance, observation_jitter,
):
    slab = ensemble[0]
    own, members = slab.shape
    cycles, count = observation_variance.shape
    member_rows = members // lags
    total = spaces * own
    smem = pl.BlockSpec(memory_space=pltpu.SMEM)
    vmem = pl.BlockSpec(memory_space=pltpu.VMEM)
    hbm = pl.BlockSpec(memory_space=pltpu.HBM)
    small = [
        neighbour_shift, edge_coupling, observation_cells, observation_weight,
        observation_reading, observation_jitter,
    ]
    dma = pltpu.SemaphoreType.DMA
    analysed, retired = pl.pallas_call(
        functools.partial(smoother_kernel, lags, spaces),
        out_shape=[
            jax.ShapeDtypeStruct((own, members), BF16),
            jax.ShapeDtypeStruct((cycles, member_rows, own), BF16),
        ],
        in_specs=[smem, hbm, hbm] + [hbm] * len(small),
        out_specs=[vmem] * 2,
        scratch_shapes=[
            pltpu.VMEM((own, members), BF16),
            pltpu.VMEM((spaces, members, own), BF16),
        ]
        + [pltpu.VMEM((spaces,) + a.shape, a.dtype) for a in small]
        + [
            pltpu.VMEM((cycles, count), F32),
            pltpu.VMEM((total, total), F32),
            pltpu.VMEM((total, members), BF16),
            pltpu.VMEM((own, members), BF16),
            pltpu.VMEM((members, own), BF16),
            pltpu.VMEM((cycles, count, own), BF16),
            pltpu.VMEM((cycles, members, count), F32),
            pltpu.VMEM((lags, member_rows, own), BF16),
            pltpu.VMEM((member_rows, own), BF16),
            pltpu.VMEM((cycles, lags, count, own), BF16),
            dma((8,)),
            dma((4, lags)), dma((4, lags)),
            dma((lags, spaces)), dma((lags, spaces)),
            dma((6, spaces)), dma((6, spaces)),
        ],
        compiler_params=pltpu.CompilerParams(
            collective_id=0, has_side_effects=True, vmem_limit_bytes=VMEM_BYTES
        ),
        name="smoother",
    )(slot_order, slab, observation_variance, *small)
    return analysed[None], retired


def solution(mesh):
    in_specs = (
        P("lag", "space", None),
        P(),
        P(None, "space"),
        P(None, "space"),
        P(None, None, "space"),
        P(None, None, "space"),
        P(None, "space"),
        P(),
        P(None, "space", None),
    )
    out_specs = (P("lag", "space", None), P(None, "lag", "space"))
    return jax.shard_map(
        functools.partial(on_device, mesh.shape["lag"], mesh.shape["space"]),
        mesh=mesh, in_specs=in_specs, out_specs=out_specs, check_vma=False,
    )
```

```python
import functools
import jax
import jax.numpy as jnp
from jax import lax
from jax.experimental import pallas as pl
from jax.experimental.pallas import tpu as pltpu
from jax.sharding import PartitionSpec as P

FC_STEPS = 4
MESH = pl.DeviceIdType.MESH
VMEM_BYTES = 64 * 1024 * 1024
F32 = jnp.float32
BF16 = jnp.bfloat16


def dot(a, b):
    return jnp.dot(a, b, preferred_element_type=F32)


def parts_of(value, count):
    parts = []
    for _ in range(count):
        part = value.astype(BF16)
        parts.append(part)
        value = value - part.astype(F32)
    return parts


def dot_parts(value, right, count):
    total = None
    for part in parts_of(value, count):
        term = dot(part, right)
        total = term if total is None else total + term
    return total


def iota(shape, dim):
    return lax.broadcasted_iota(jnp.int32, shape, dim)


def column_of(row):
    n = row.shape[1]
    return jnp.sum(
        jnp.where(iota((n, n), 0) == iota((n, n), 1), row, 0.0), axis=1, keepdims=True
    )


def inverse_of(gram):
    n = gram.shape[0]
    at_row, at_column = iota((n, n), 0), iota((n, n), 1)
    line = at_column[:1]
    for k in range(0, n, 2):
        left = jnp.broadcast_to(gram[:, k : k + 1], (n, n))
        right = jnp.broadcast_to(gram[:, k + 1 : k + 2], (n, n))
        a, b, d = left[k : k + 1], left[k + 1 : k + 2], right[k + 1 : k + 2]
        scale = 1.0 / (a * d - b * b)
        pivots = (line == k) | (line == k + 1)
        upper = jnp.where(pivots, jnp.where(line == k, 1.0, 0.0), gram[k : k + 1])
        lower = jnp.where(pivots, jnp.where(line == k, 0.0, 1.0), gram[k + 1 : k + 2])
        first = (d * upper - b * lower) * scale
        second = (a * lower - b * upper) * scale
        rest = jnp.where((at_column == k) | (at_column == k + 1), 0.0, gram)
        rest = rest - left * first - right * second
        gram = jnp.where(at_row == k, first, jnp.where(at_row == k + 1, second, rest))
    return gram


def anomaly_of(values):
    centre = jnp.mean(values, axis=1, keepdims=True)
    return (values - centre).astype(BF16)


def across_members(a, b):
    return lax.dot_general(a, b, (((1,), (1,)), ((), ())), preferred_element_type=F32)


def smoother_kernel(lags, spaces, slot_ref, slab_hbm, variance_hbm, *refs):
    small_in, refs = refs[:6], refs[6:]
    out_ref, retired_ref, slab_ref, whole_ref, refs = refs[0], refs[1], refs[2], refs[3], refs[4:]
    small_all, refs = refs[:6], refs[6:]
    (
        variance_ref, matrix, forecast, anomaly, turned, cross_out, solved_turned, landing,
        landing_cross, local_sem, send_l, recv_l, send_3, recv_3, send_s, recv_s,
    ) = refs
    shift_ref, coupling_ref, cells_ref, weight_ref, reading_ref, jitter_ref = small_all
    lag, space = lax.axis_index("lag"), lax.axis_index("space")
    own, members = slab_ref.shape
    total = spaces * own
    cycles = variance_ref.shape[0]
    corners, wanted = cells_ref.shape[2], cells_ref.shape[3]
    member_rows = members // lags

    def member_place(block):
        return pl.ds(pl.multiple_of(block * member_rows, member_rows), member_rows)

    def lag_at(step):
        return lax.rem(lag + step, lags)

    def space_at(step):
        return lax.rem(space + step, spaces)

    def send_lag(kind, step, source, target):
        copy = pltpu.make_async_remote_copy(
            src_ref=source,
            dst_ref=target,
            send_sem=send_l.at[kind, step],
            recv_sem=recv_l.at[kind, step],
            device_id=(lag_at(step), space),
            device_id_type=MESH,
        )
        copy.start()
        return copy

    local = [
        pltpu.make_async_copy(slab_hbm, slab_ref, local_sem.at[6]),
        pltpu.make_async_copy(variance_hbm, variance_ref, local_sem.at[7]),
    ]
    for item in range(6):
        local.append(
            pltpu.make_async_copy(small_in[item], small_all[item].at[space], local_sem.at[item])
        )
    for copy in local:
        copy.start()
    barrier = pltpu.get_barrier_semaphore()
    for step in range(1, lags):
        pl.semaphore_signal(barrier, inc=1, device_id=(lag_at(step), space), device_id_type=MESH)
    for step in range(1, spaces):
        pl.semaphore_signal(barrier, inc=1, device_id=(lag, space_at(step)), device_id_type=MESH)
    local[0].wait()
    turned[...] = slab_ref[...].astype(F32).T.astype(BF16)
    pl.semaphore_wait(barrier, lags - 1 + spaces - 1)

    scatter = [
        send_lag(0, step, turned.at[member_place(lag_at(step))], landing.at[step])
        for step in range(1, lags)
    ]
    small = []
    for step in range(1, spaces):
        for item in range(6):
            copy = pltpu.make_async_remote_copy(
                src_ref=small_in[item],
                dst_ref=small_all[item].at[space],
                send_sem=send_s.at[item, step],
                recv_sem=recv_s.at[item, step],
                device_id=(lag, space_at(step)),
                device_id_type=MESH,
            )
            copy.start()
            small.append(copy)
    for copy in local[1:]:
        copy.wait()
    for copy in small:
        copy.wait()

    source_cell = iota((total, own), 0)
    for part in range(spaces):
        cell = iota((total, own), 1) + part * own
        kept = jnp.zeros((1, own), F32)
        entry = jnp.zeros((total, own), F32)
        for k in range(shift_ref.shape[1]):
            weight = coupling_ref[part, k : k + 1, :]
            offset = shift_ref[part, k : k + 1, :]
            entry = entry + jnp.where(source_cell - cell == offset, weight, 0.0)
            kept = kept + weight
        entry = entry + jnp.where(source_cell == cell, 1.0 - kept, 0.0)
        matrix[:, part * own : (part + 1) * own] = entry
    power = FC_STEPS
    one = matrix[...]
    while power > 1:
        one = jnp.dot(one, one, precision=lax.Precision.HIGHEST, preferred_element_type=F32)
        power //= 2
    operator = parts_of(one.T, 2)
    holds, readings = [], []
    for cycle in range(cycles):
        hold_cycle, reading_cycle = [], []
        for part in range(spaces):
            hold = jnp.zeros((own, wanted), F32)
            for q in range(corners):
                hold = hold + jnp.where(
                    iota((own, wanted), 0) == cells_ref[part, cycle, q : q + 1, :],
                    weight_ref[part, cycle, q : q + 1, :],
                    0.0,
                )
            hold_cycle.append(hold.T)
            variance = variance_ref[cycle : cycle + 1, part * wanted : (part + 1) * wanted]
            reading_cycle.append(
                column_of(reading_ref[part, cycle : cycle + 1, :])
                + jnp.sqrt(column_of(variance)) * jitter_ref[part, cycle]
            )
        holds.append(hold_cycle)
        readings.append(jnp.concatenate(reading_cycle, axis=0))

    source, target_0, target_1 = slot_ref[0], slot_ref[lags - 1], slot_ref[lags - 2]
    mine = turned[member_place(lag)]
    block = mine
    for step in range(1, lags):
        scatter[step - 1].wait_recv()
        block = jnp.where(lag_at(lags - step) == source, landing[step], block)
    whole_ref[space, member_place(lag)] = block

    inner = 4 if lags % 4 == 0 else 1
    outers = lags // inner
    outer, within = lag // inner, lag % inner

    def lag_near(far, near):
        return lax.rem(outer + far, outers) * inner + lax.rem(within + near, inner)

    def hand_on(far, near, position, to):
        spot = whole_ref.at[space, member_place(position)]
        copy = pltpu.make_async_remote_copy(
            src_ref=spot,
            dst_ref=spot,
            send_sem=send_l.at[1, far * inner + near],
            recv_sem=recv_l.at[1, far * inner + near],
            device_id=(to, space),
            device_id_type=MESH,
        )
        copy.start()
        gather[far, near] = copy

    forward = []

    def across_spaces(step, position):
        spot = whole_ref.at[space, member_place(position)]
        for aside in range(1, spaces):
            copy = pltpu.make_async_remote_copy(
                src_ref=spot,
                dst_ref=spot,
                send_sem=send_3.at[step, aside],
                recv_sem=recv_3.at[step, aside],
                device_id=(lag, space_at(aside)),
                device_id_type=MESH,
            )
            copy.start()
            forward.append(copy)

    gather = {}
    for far in range(1, outers):
        hand_on(far, 0, lag, lag_near(far, 0))
    for near in range(1, inner):
        hand_on(0, near, lag, lag_near(0, near))
    across_spaces(0, lag)
    first, second = mine, mine
    for step in range(1, lags):
        sender = lag_at(lags - step)
        first = jnp.where(sender == target_0, landing[step], first)
        second = jnp.where(sender == target_1, landing[step], second)
    anomaly[...] = anomaly_of(slab_ref[...].astype(F32))
    for far in range(1, outers):
        gather[far, 0].wait_recv()
        position = lag_near(outers - far, 0)
        for near in range(1, inner):
            hand_on(far, near, position, lag_near(0, near))
        across_spaces(far * inner, position)
    for far in range(outers):
        for near in range(1, inner):
            gather[far, near].wait_recv()
            across_spaces(far * inner + near, lag_near(outers - far, inner - near))
    for copy in forward:
        copy.wait_recv()

    def observed(cycle, ahead):
        measured = jnp.concatenate(
            [
                dot_parts(holds[cycle][part], ahead[part * own : (part + 1) * own], 3)
                for part in range(spaces)
            ],
            axis=0,
        )
        return anomaly_of(measured), (readings[cycle] - measured).astype(BF16)

    def solve(cycle, spread, innovation):
        gram = across_members(spread, spread)
        n = gram.shape[0]
        gram = gram + jnp.where(
            iota((n, n), 0) == iota((n, n), 1),
            (members - 1) * variance_ref[cycle : cycle + 1, :],
            0.0,
        )
        return dot_parts(inverse_of(gram), innovation, 3).astype(BF16)

    def own_rows(value):
        forecast[...] = value
        return forecast[pl.ds(pl.multiple_of(space * own, own), own), :]

    def send_cross(cycle, cross):
        cross_out[cycle] = cross.T.astype(BF16)
        return [
            send_lag(2 + cycle, step, cross_out.at[cycle], landing_cross.at[cycle, step])
            for step in range(1, lags)
        ]

    def chosen_cross(cycle, target):
        value = cross_out[cycle]
        for step in range(1, lags):
            value = jnp.where(lag_at(lags - step) == target, landing_cross[cycle, step], value)
        return value

    def retire(cycle, values, solved, cross):
        solved_turned[cycle] = solved.astype(F32).T
        weights = solved_turned[cycle, member_place(lag)].astype(BF16)
        return (values.astype(F32) + dot(weights, cross)).astype(BF16)

    newest = jnp.concatenate([whole_ref[part] for part in range(spaces)], axis=1)
    ahead = (across_members(operator[0], newest) + across_members(operator[1], newest)).astype(BF16)
    spread, innovation = observed(0, ahead)
    cross = across_members(anomaly[...], spread)
    crosses = send_cross(0, cross)
    ahead_f = ahead.astype(F32)
    cross_ahead = across_members(anomaly_of(ahead_f), spread)
    solved_0 = solve(0, spread, innovation)
    newest = (ahead_f + dot_parts(cross_ahead, solved_0, 2)).astype(BF16)
    updated = (slab_ref[...].astype(F32) + dot_parts(cross, solved_0, 2)).astype(BF16)
    state = jnp.where(lag == target_0, own_rows(newest), updated).astype(F32)

    ahead = (dot(operator[0], newest) + dot(operator[1], newest)).astype(BF16)
    spread, innovation = observed(1, ahead)
    cross = across_members(anomaly_of(state), spread)
    crosses_1 = send_cross(1, cross)
    ahead_own = own_rows(ahead).astype(F32)
    cross_ahead = across_members(anomaly_of(ahead_own), spread)
    solved_1 = solve(1, spread, innovation)
    base = jnp.where(lag == target_1, ahead_own, state)
    cross = jnp.where(lag == target_1, cross_ahead, cross)
    out_ref[...] = (base + dot_parts(cross, solved_1, 2)).astype(BF16)

    for copy in crosses:
        copy.wait_recv()
    retired_ref[0] = retire(0, first, solved_0, chosen_cross(0, target_0))
    second = retire(0, second, solved_0, chosen_cross(0, target_1))
    for copy in crosses_1:
        copy.wait_recv()
    retired_ref[1] = retire(1, second, solved_1, chosen_cross(1, target_1))
    for copy in scatter + list(gather.values()) + forward + crosses + crosses_1:
        copy.wait_send()


def keep_kernel(analysed_ref, retired_ref, analysed_out, retired_out, sems):
    copies = [
        pltpu.make_async_copy(analysed_ref, analysed_out, sems.at[0]),
        pltpu.make_async_copy(retired_ref, retired_out, sems.at[1]),
    ]
    for copy in copies:
        copy.start()
    for copy in copies:
        copy.wait()


def on_device(
    lags, spaces, ensemble, slot_order, neighbour_shift, edge_coupling, observation_cells,
    observation_weight, observation_reading, observation_variance, observation_jitter,
):
    slab = ensemble[0]
    own, members = slab.shape
    cycles, count = observation_variance.shape
    member_rows = members // lags
    total = spaces * own
    smem = pl.BlockSpec(memory_space=pltpu.SMEM)
    vmem = pl.BlockSpec(memory_space=pltpu.VMEM)
    hbm = pl.BlockSpec(memory_space=pltpu.HBM)
    small = [
        neighbour_shift, edge_coupling, observation_cells, observation_weight,
        observation_reading, observation_jitter,
    ]
    dma = pltpu.SemaphoreType.DMA
    analysed, retired = pl.pallas_call(
        functools.partial(smoother_kernel, lags, spaces),
        out_shape=[
            jax.ShapeDtypeStruct((own, members), BF16),
            jax.ShapeDtypeStruct((cycles, member_rows, own), BF16),
        ],
        in_specs=[smem, hbm, hbm] + [hbm] * len(small),
        out_specs=[vmem] * 2,
        scratch_shapes=[
            pltpu.VMEM((own, members), BF16),
            pltpu.VMEM((spaces, members, own), BF16),
        ]
        + [pltpu.VMEM((spaces,) + a.shape, a.dtype) for a in small]
        + [
            pltpu.VMEM((cycles, count), F32),
            pltpu.VMEM((total, total), F32),
            pltpu.VMEM((total, members), BF16),
            pltpu.VMEM((own, members), BF16),
            pltpu.VMEM((members, own), BF16),
            pltpu.VMEM((cycles, count, own), BF16),
            pltpu.VMEM((cycles, members, count), F32),
            pltpu.VMEM((lags, member_rows, own), BF16),
            pltpu.VMEM((cycles, lags, count, own), BF16),
            dma((8,)),
            dma((4, lags)), dma((4, lags)),
            dma((lags, spaces)), dma((lags, spaces)),
            dma((6, spaces)), dma((6, spaces)),
        ],
        compiler_params=pltpu.CompilerParams(
            collective_id=0, has_side_effects=True, vmem_limit_bytes=VMEM_BYTES
        ),
        name="smoother",
    )(slot_order, slab, observation_variance, *small)
    analysed, retired = pl.pallas_call(
        keep_kernel,
        out_shape=[
            jax.ShapeDtypeStruct(analysed.shape, BF16),
            jax.ShapeDtypeStruct(retired.shape, BF16),
        ],
        in_specs=[hbm] * 2,
        out_specs=[hbm] * 2,
        scratch_shapes=[dma((2,))],
        compiler_params=pltpu.CompilerParams(vmem_limit_bytes=VMEM_BYTES),
        name="keep",
    )(analysed, retired)
    return analysed[None], retired


def solution(mesh):
    in_specs = (
        P("lag", "space", None),
        P(),
        P(None, "space"),
        P(None, "space"),
        P(None, None, "space"),
        P(None, None, "space"),
        P(None, "space"),
        P(),
        P(None, "space", None),
    )
    out_specs = (P("lag", "space", None), P(None, "lag", "space"))
    return jax.shard_map(
        functools.partial(on_device, mesh.shape["lag"], mesh.shape["space"]),
        mesh=mesh, in_specs=in_specs, out_specs=out_specs, check_vma=False,
    )
```

```python
import functools
import jax
import jax.numpy as jnp
from jax import lax
from jax.experimental import pallas as pl
from jax.experimental.pallas import tpu as pltpu
from jax.sharding import PartitionSpec as P

FC_STEPS = 4
MESH = pl.DeviceIdType.MESH
VMEM_BYTES = 64 * 1024 * 1024
F32 = jnp.float32
BF16 = jnp.bfloat16


def dot(a, b):
    return jnp.dot(a, b, preferred_element_type=F32)


def parts_of(value, count):
    parts = []
    for _ in range(count):
        part = value.astype(BF16)
        parts.append(part)
        value = value - part.astype(F32)
    return parts


def dot_parts(value, right, count):
    total = None
    for part in parts_of(value, count):
        term = dot(part, right)
        total = term if total is None else total + term
    return total


def iota(shape, dim):
    return lax.broadcasted_iota(jnp.int32, shape, dim)


def column_of(row):
    n = row.shape[1]
    return jnp.sum(
        jnp.where(iota((n, n), 0) == iota((n, n), 1), row, 0.0), axis=1, keepdims=True
    )


def inverse_of(gram):
    n = gram.shape[0]
    at_row, at_column = iota((n, n), 0), iota((n, n), 1)
    line = at_column[:1]
    for k in range(0, n, 2):
        left = jnp.broadcast_to(gram[:, k : k + 1], (n, n))
        right = jnp.broadcast_to(gram[:, k + 1 : k + 2], (n, n))
        a, b, d = left[k : k + 1], left[k + 1 : k + 2], right[k + 1 : k + 2]
        scale = 1.0 / (a * d - b * b)
        pivots = (line == k) | (line == k + 1)
        upper = jnp.where(pivots, jnp.where(line == k, 1.0, 0.0), gram[k : k + 1])
        lower = jnp.where(pivots, jnp.where(line == k, 0.0, 1.0), gram[k + 1 : k + 2])
        first = (d * upper - b * lower) * scale
        second = (a * lower - b * upper) * scale
        rest = jnp.where((at_column == k) | (at_column == k + 1), 0.0, gram)
        rest = rest - left * first - right * second
        gram = jnp.where(at_row == k, first, jnp.where(at_row == k + 1, second, rest))
    return gram


def anomaly_of(values):
    centre = jnp.mean(values, axis=1, keepdims=True)
    return (values - centre).astype(BF16)


def across_members(a, b):
    return lax.dot_general(a, b, (((1,), (1,)), ((), ())), preferred_element_type=F32)


def smoother_kernel(lags, spaces, slot_ref, slab_hbm, variance_hbm, *refs):
    small_in, refs = refs[:6], refs[6:]
    out_ref, retired_ref, slab_ref, whole_ref, refs = refs[0], refs[1], refs[2], refs[3], refs[4:]
    small_all, refs = refs[:6], refs[6:]
    (
        variance_ref, matrix, forecast, anomaly, turned, cross_out, solved_turned, landing,
        landing_cross, local_sem, send_l, recv_l, send_3, recv_3, send_s, recv_s,
    ) = refs
    shift_ref, coupling_ref, cells_ref, weight_ref, reading_ref, jitter_ref = small_all
    lag, space = lax.axis_index("lag"), lax.axis_index("space")
    own, members = slab_ref.shape
    total = spaces * own
    cycles = variance_ref.shape[0]
    corners, wanted = cells_ref.shape[2], cells_ref.shape[3]
    member_rows = members // lags

    def member_place(block):
        return pl.ds(pl.multiple_of(block * member_rows, member_rows), member_rows)

    def lag_at(step):
        return lax.rem(lag + step, lags)

    def space_at(step):
        return lax.rem(space + step, spaces)

    def send_lag(kind, step, source, target):
        copy = pltpu.make_async_remote_copy(
            src_ref=source,
            dst_ref=target,
            send_sem=send_l.at[kind, step],
            recv_sem=recv_l.at[kind, step],
            device_id=(lag_at(step), space),
            device_id_type=MESH,
        )
        copy.start()
        return copy

    local = [
        pltpu.make_async_copy(slab_hbm, slab_ref, local_sem.at[6]),
        pltpu.make_async_copy(variance_hbm, variance_ref, local_sem.at[7]),
    ]
    for item in range(6):
        local.append(
            pltpu.make_async_copy(small_in[item], small_all[item].at[space], local_sem.at[item])
        )
    for copy in local:
        copy.start()
    barrier = pltpu.get_barrier_semaphore()
    for step in range(1, lags):
        pl.semaphore_signal(barrier, inc=1, device_id=(lag_at(step), space), device_id_type=MESH)
    for step in range(1, spaces):
        pl.semaphore_signal(barrier, inc=1, device_id=(lag, space_at(step)), device_id_type=MESH)
    local[0].wait()
    turned[...] = slab_ref[...].astype(F32).T.astype(BF16)
    pl.semaphore_wait(barrier, lags - 1 + spaces - 1)

    scatter = [
        send_lag(0, step, turned.at[member_place(lag_at(step))], landing.at[step])
        for step in range(1, lags)
    ]
    small = []
    for step in range(1, spaces):
        for item in range(6):
            copy = pltpu.make_async_remote_copy(
                src_ref=small_in[item],
                dst_ref=small_all[item].at[space],
                send_sem=send_s.at[item, step],
                recv_sem=recv_s.at[item, step],
                device_id=(lag, space_at(step)),
                device_id_type=MESH,
            )
            copy.start()
            small.append(copy)
    for copy in local[1:]:
        copy.wait()
    for copy in small:
        copy.wait()

    source_cell = iota((total, own), 0)
    for part in range(spaces):
        cell = iota((total, own), 1) + part * own
        kept = jnp.zeros((1, own), F32)
        entry = jnp.zeros((total, own), F32)
        for k in range(shift_ref.shape[1]):
            weight = coupling_ref[part, k : k + 1, :]
            offset = shift_ref[part, k : k + 1, :]
            entry = entry + jnp.where(source_cell - cell == offset, weight, 0.0)
            kept = kept + weight
        entry = entry + jnp.where(source_cell == cell, 1.0 - kept, 0.0)
        matrix[:, part * own : (part + 1) * own] = entry
    power = FC_STEPS
    one = matrix[...]
    while power > 1:
        one = jnp.dot(one, one, precision=lax.Precision.HIGHEST, preferred_element_type=F32)
        power //= 2
    operator = parts_of(one.T, 2)
    holds, readings = [], []
    for cycle in range(cycles):
        hold_cycle, reading_cycle = [], []
        for part in range(spaces):
            hold = jnp.zeros((own, wanted), F32)
            for q in range(corners):
                hold = hold + jnp.where(
                    iota((own, wanted), 0) == cells_ref[part, cycle, q : q + 1, :],
                    weight_ref[part, cycle, q : q + 1, :],
                    0.0,
                )
            hold_cycle.append(hold.T)
            variance = variance_ref[cycle : cycle + 1, part * wanted : (part + 1) * wanted]
            reading_cycle.append(
                column_of(reading_ref[part, cycle : cycle + 1, :])
                + jnp.sqrt(column_of(variance)) * jitter_ref[part, cycle]
            )
        holds.append(hold_cycle)
        readings.append(jnp.concatenate(reading_cycle, axis=0))

    source, target_0, target_1 = slot_ref[0], slot_ref[lags - 1], slot_ref[lags - 2]
    mine = turned[member_place(lag)]
    block = mine
    for step in range(1, lags):
        scatter[step - 1].wait_recv()
        block = jnp.where(lag_at(lags - step) == source, landing[step], block)
    whole_ref[space, member_place(lag)] = block

    inner = 4 if lags % 4 == 0 else 1
    outers = lags // inner
    outer, within = lag // inner, lag % inner

    def lag_near(far, near):
        return lax.rem(outer + far, outers) * inner + lax.rem(within + near, inner)

    def hand_on(far, near, position, to):
        spot = whole_ref.at[space, member_place(position)]
        copy = pltpu.make_async_remote_copy(
            src_ref=spot,
            dst_ref=spot,
            send_sem=send_l.at[1, far * inner + near],
            recv_sem=recv_l.at[1, far * inner + near],
            device_id=(to, space),
            device_id_type=MESH,
        )
        copy.start()
        gather[far, near] = copy

    forward = []

    def across_spaces(step, position):
        spot = whole_ref.at[space, member_place(position)]
        for aside in range(1, spaces):
            copy = pltpu.make_async_remote_copy(
                src_ref=spot,
                dst_ref=spot,
                send_sem=send_3.at[step, aside],
                recv_sem=recv_3.at[step, aside],
                device_id=(lag, space_at(aside)),
                device_id_type=MESH,
            )
            copy.start()
            forward.append(copy)

    gather = {}
    for far in range(1, outers):
        hand_on(far, 0, lag, lag_near(far, 0))
    for near in range(1, inner):
        hand_on(0, near, lag, lag_near(0, near))
    across_spaces(0, lag)
    first, second = mine, mine
    for step in range(1, lags):
        sender = lag_at(lags - step)
        first = jnp.where(sender == target_0, landing[step], first)
        second = jnp.where(sender == target_1, landing[step], second)
    anomaly[...] = anomaly_of(slab_ref[...].astype(F32))
    for far in range(1, outers):
        gather[far, 0].wait_recv()
        position = lag_near(outers - far, 0)
        for near in range(1, inner):
            hand_on(far, near, position, lag_near(0, near))
        across_spaces(far * inner, position)
    for far in range(outers):
        for near in range(1, inner):
            gather[far, near].wait_recv()
            across_spaces(far * inner + near, lag_near(outers - far, inner - near))
    for copy in forward:
        copy.wait_recv()

    def observed(cycle, ahead):
        measured = jnp.concatenate(
            [
                dot_parts(holds[cycle][part], ahead[part * own : (part + 1) * own], 3)
                for part in range(spaces)
            ],
            axis=0,
        )
        return anomaly_of(measured), (readings[cycle] - measured).astype(BF16)

    def solve(cycle, spread, innovation):
        gram = across_members(spread, spread)
        n = gram.shape[0]
        gram = gram + jnp.where(
            iota((n, n), 0) == iota((n, n), 1),
            (members - 1) * variance_ref[cycle : cycle + 1, :],
            0.0,
        )
        return dot_parts(inverse_of(gram), innovation, 3).astype(BF16)

    def own_rows(value):
        forecast[...] = value
        return forecast[pl.ds(pl.multiple_of(space * own, own), own), :]

    def send_cross(cycle, cross):
        cross_out[cycle] = cross.T.astype(BF16)
        return [
            send_lag(2 + cycle, step, cross_out.at[cycle], landing_cross.at[cycle, step])
            for step in range(1, lags)
        ]

    def chosen_cross(cycle, target):
        value = cross_out[cycle]
        for step in range(1, lags):
            value = jnp.where(lag_at(lags - step) == target, landing_cross[cycle, step], value)
        return value

    def retire(cycle, values, solved, cross):
        solved_turned[cycle] = solved.astype(F32).T
        weights = solved_turned[cycle, member_place(lag)].astype(BF16)
        return (values.astype(F32) + dot(weights, cross)).astype(BF16)

    newest = jnp.concatenate([whole_ref[part] for part in range(spaces)], axis=1)
    ahead = (across_members(operator[0], newest) + across_members(operator[1], newest)).astype(BF16)
    spread, innovation = observed(0, ahead)
    cross = across_members(anomaly[...], spread)
    crosses = send_cross(0, cross)
    ahead_f = ahead.astype(F32)
    cross_ahead = across_members(anomaly_of(ahead_f), spread)
    solved_0 = solve(0, spread, innovation)
    newest = (ahead_f + dot_parts(cross_ahead, solved_0, 2)).astype(BF16)
    updated = (slab_ref[...].astype(F32) + dot_parts(cross, solved_0, 2)).astype(BF16)
    state = jnp.where(lag == target_0, own_rows(newest), updated).astype(F32)

    ahead = (dot(operator[0], newest) + dot(operator[1], newest)).astype(BF16)
    spread, innovation = observed(1, ahead)
    cross = across_members(anomaly_of(state), spread)
    crosses_1 = send_cross(1, cross)
    ahead_own = own_rows(ahead).astype(F32)
    cross_ahead = across_members(anomaly_of(ahead_own), spread)
    solved_1 = solve(1, spread, innovation)
    base = jnp.where(lag == target_1, ahead_own, state)
    cross = jnp.where(lag == target_1, cross_ahead, cross)
    out_ref[...] = (base + dot_parts(cross, solved_1, 2)).astype(BF16)

    for copy in crosses:
        copy.wait_recv()
    retired_ref[0] = retire(0, first, solved_0, chosen_cross(0, target_0))
    second = retire(0, second, solved_0, chosen_cross(0, target_1))
    for copy in crosses_1:
        copy.wait_recv()
    retired_ref[1] = retire(1, second, solved_1, chosen_cross(1, target_1))
    for copy in scatter + list(gather.values()) + forward + crosses + crosses_1:
        copy.wait_send()


def keep_kernel(analysed_ref, retired_ref, analysed_out, retired_out):
    analysed_out[...] = analysed_ref[...]
    retired_out[...] = retired_ref[...]


def on_device(
    lags, spaces, ensemble, slot_order, neighbour_shift, edge_coupling, observation_cells,
    observation_weight, observation_reading, observation_variance, observation_jitter,
):
    slab = ensemble[0]
    own, members = slab.shape
    cycles, count = observation_variance.shape
    member_rows = members // lags
    total = spaces * own
    smem = pl.BlockSpec(memory_space=pltpu.SMEM)
    vmem = pl.BlockSpec(memory_space=pltpu.VMEM)
    hbm = pl.BlockSpec(memory_space=pltpu.HBM)
    small = [
        neighbour_shift, edge_coupling, observation_cells, observation_weight,
        observation_reading, observation_jitter,
    ]
    dma = pltpu.SemaphoreType.DMA
    analysed, retired = pl.pallas_call(
        functools.partial(smoother_kernel, lags, spaces),
        out_shape=[
            jax.ShapeDtypeStruct((own, members), BF16),
            jax.ShapeDtypeStruct((cycles, member_rows, own), BF16),
        ],
        in_specs=[smem, hbm, hbm] + [hbm] * len(small),
        out_specs=[vmem] * 2,
        scratch_shapes=[
            pltpu.VMEM((own, members), BF16),
            pltpu.VMEM((spaces, members, own), BF16),
        ]
        + [pltpu.VMEM((spaces,) + a.shape, a.dtype) for a in small]
        + [
            pltpu.VMEM((cycles, count), F32),
            pltpu.VMEM((total, total), F32),
            pltpu.VMEM((total, members), BF16),
            pltpu.VMEM((own, members), BF16),
            pltpu.VMEM((members, own), BF16),
            pltpu.VMEM((cycles, count, own), BF16),
            pltpu.VMEM((cycles, members, count), F32),
            pltpu.VMEM((lags, member_rows, own), BF16),
            pltpu.VMEM((cycles, lags, count, own), BF16),
            dma((8,)),
            dma((4, lags)), dma((4, lags)),
            dma((lags, spaces)), dma((lags, spaces)),
            dma((6, spaces)), dma((6, spaces)),
        ],
        compiler_params=pltpu.CompilerParams(
            collective_id=0, has_side_effects=True, vmem_limit_bytes=VMEM_BYTES
        ),
        name="smoother",
    )(slot_order, slab, observation_variance, *small)
    analysed, retired = pl.pallas_call(
        keep_kernel,
        out_shape=[
            jax.ShapeDtypeStruct(analysed.shape, BF16),
            jax.ShapeDtypeStruct(retired.shape, BF16),
        ],
        in_specs=[vmem] * 2,
        out_specs=[vmem] * 2,
        compiler_params=pltpu.CompilerParams(vmem_limit_bytes=VMEM_BYTES),
        name="keep",
    )(analysed, retired)
    return analysed[None], retired


def solution(mesh):
    in_specs = (
        P("lag", "space", None),
        P(),
        P(None, "space"),
        P(None, "space"),
        P(None, None, "space"),
        P(None, None, "space"),
        P(None, "space"),
        P(),
        P(None, "space", None),
    )
    out_specs = (P("lag", "space", None), P(None, "lag", "space"))
    return jax.shard_map(
        functools.partial(on_device, mesh.shape["lag"], mesh.shape["space"]),
        mesh=mesh, in_specs=in_specs, out_specs=out_specs, check_vma=False,
    )
```
